32 devices in a mesh: parts: 2 (over x), gx: 4 (over y, core), ka: 4 (over z).
Axes of the slice: x: 2, y: 2, z: 4, core: 2. Of those that a mesh axis runs over, the one named last changes fastest.
Arguments:
- bloch_modes: float32 [16, 2, 2, 3, 32, 128, 128], P(('parts', 'ka'), None, None, None, 'gx'), parts along dimension 0, may hold values from -104 to 104, as said below
- permittivity: float32 [64, 128, 128], P(('parts', 'gx')), parts along dimension 0, may hold values from 1 to 4
- bloch_phase: float32 [8], P('ka'), may hold values from -3.140625 to 3.140625
- edge_side: int32 [8, 2], P('ka'), may hold values from 0 to 1, as said below
Outputs:
- filtered_gradient: float32 [64, 128, 128], P(('parts', 'gx'), 'ka'), parts along dimension 0
- omega_squared: float32 [16, 2], P(('parts', 'ka')), parts along dimension 0
The draws below stay inside these ranges and needn't reach their ends.
There are 2 independent parts, one for each index of `parts`. The reference program is written for one: setup_inputs(seed, part) draws one part's arguments, and reference() takes and returns one part's arrays. A program takes and returns all parts, laid end to end along the dimension named above; an argument that names none is the same for every part. Nothing has to cross between parts.
Inputs may be any that keep to these rules, and one draw needn't show every extreme that they name: `bloch_modes`: bloch mode fields. `edge_side`: at each k-point one of the 2 bands is the upper edge and the other the lower.
All inputs are finite; a program needn't handle non-finite values.
Results may differ from the reference program's by a relative error of at most 0.0003.
Values sent between devices are 32-bit elements; how exact they have to be, the bound alone decides.
A program may use at most 128 MiB of HBM per device.

```python
import math
import jax
import jax.numpy as jnp
from jax import lax

BANDS = 2
NY = 128
NZ = 128
SWEEPS = 8
KPTS = 8
NX = 32


def draw_bloch_modes(key, part):
    key = jax.random.fold_in(key, 7)
    key_base, key_rows, key_cols = jax.random.split(key, 3)
    full_shape = (KPTS, BANDS, 2, 3, NX, NY, NZ)
    position = jnp.arange(NX, dtype=jnp.float32) / max(NX - 1, 1)
    base_values = jnp.clip(jax.random.normal(key_base, full_shape, jnp.float32), -6.0, 6.0)
    profile = jnp.sqrt(1.0 + 2.0 * position)
    row_scale = jnp.exp(jax.random.uniform(key_rows, (NY,), jnp.float32, 0.0, 1.1512925))
    col_scale = jnp.exp(jax.random.uniform(key_cols, (NZ,), jnp.float32, 0.0, 1.1512925))
    return base_values * profile[:, None, None] * row_scale[:, None] * col_scale


def draw_edge_side(key, part):
    key = jax.random.fold_in(key, 11)
    first_band = jax.random.randint(key, (KPTS,), 0, 2, dtype=jnp.int32)
    return jnp.stack([first_band, 1 - first_band], axis=1).astype(jnp.int32)


def steps_of(key, dims, cuts, smallest, largest):
    def one(dim, shards_of):
        steps = jax.random.uniform(jax.random.fold_in(jax.random.fold_in(key, 6), dim), (shards_of,), jnp.float32, smallest / len(cuts), largest / len(cuts))
        return jnp.repeat(jnp.exp(steps), dims[dim] // shards_of).reshape((-1,) + (1,) * (len(dims) - dim - 1))

    gain = one(*cuts[0])
    for cut in cuts[1:]:
        gain = gain * one(*cut)
    return gain


def setup_inputs(seed: int = 0, part: int = 0) -> dict:
    seeds = jax.random.split(jax.random.key(seed), 5)
    part_splits = jax.random.split(jax.random.fold_in(seeds[4], part), 5)
    bloch_modes = draw_bloch_modes(jax.random.fold_in(jax.random.fold_in(seeds[4], part), 71), part)
    permittivity = jnp.clip(jnp.exp(math.log(4.0) - 1.3862944 * jax.random.uniform(part_splits[1], (NX, NY, NZ), jnp.float32) ** steps_of(part_splits[1], (NX, NY, NZ), ((0, 4),), -0.2, 0.2)), 1.0, 4.0)
    bloch_phase = jnp.clip(jax.random.uniform(seeds[2], (KPTS,), jnp.float32, -3.140625, 3.140625), -3.140625, 3.140625)
    edge_side = draw_edge_side(jax.random.fold_in(seeds[4], 71), part)
    return {"bloch_modes": bloch_modes, "permittivity": permittivity, "bloch_phase": bloch_phase, "edge_side": edge_side}


filter_weight = 4.0


def lower_z(values_in):
    zero_plane = jnp.zeros_like(values_in[..., :1])
    return jnp.concatenate([zero_plane, values_in[..., :-1]], axis=-1)


def upper_z(values_in):
    zero_plane = jnp.zeros_like(values_in[..., :1])
    return jnp.concatenate([values_in[..., 1:], zero_plane], axis=-1)


def mode_curl(field_h, phase_angle):
    cosine = jnp.cos(phase_angle)
    sine_part = jnp.sin(phase_angle)
    last_plane = field_h[:, :, :, -1:]
    rotated = jnp.stack([last_plane[:, 0] * cosine + last_plane[:, 1] * sine_part,
                         last_plane[:, 1] * cosine - last_plane[:, 0] * sine_part], axis=1)
    before_x = jnp.concatenate([rotated, field_h[:, :, :, :-1]], axis=3)
    diff_x = field_h - before_x
    diff_y = field_h - jnp.roll(field_h, 1, axis=4)
    diff_z = field_h - lower_z(field_h)
    curl_x = diff_y[:, :, 2] - diff_z[:, :, 1]
    curl_y = diff_z[:, :, 0] - diff_x[:, :, 2]
    curl_z = diff_x[:, :, 1] - diff_y[:, :, 0]
    return jnp.sum(curl_x * curl_x + curl_y * curl_y + curl_z * curl_z, axis=1)


def relax_whole(density, gradient):
    neighbours = jnp.roll(density, 1, axis=0) + jnp.roll(density, -1, axis=0)
    neighbours = neighbours + jnp.roll(density, 1, axis=1) + jnp.roll(density, -1, axis=1)
    neighbours = neighbours + lower_z(density) + upper_z(density)
    return (gradient + filter_weight * neighbours) / (1.0 + 6.0 * filter_weight)


def reference(bloch_modes, permittivity, bloch_phase, edge_side):
    inverse = 1.0 / permittivity
    cell_count = NX * NY * NZ

    def per_point(accumulated, inputs):
        field_h, phase_angle, edge_value = inputs
        squared = mode_curl(field_h, phase_angle)
        mode_energy = jnp.sum(squared * inverse, axis=(1, 2, 3))
        mode_norm = jnp.sum(field_h * field_h, axis=(1, 2, 3, 4, 5))
        mode_weight = -(2.0 * edge_value.astype(jnp.float32) - 1.0) * cell_count / mode_norm
        accumulated = accumulated + jnp.sum(mode_weight[:, None, None, None] * squared, axis=0)
        return accumulated, mode_energy / mode_norm

    start = jnp.zeros((NX, NY, NZ), jnp.float32)
    summed, omega_squared = lax.scan(per_point, start, (bloch_modes, bloch_phase, edge_side))
    gradient = summed * inverse * inverse
    density = gradient
    for sweep_index in range(SWEEPS):
        density = relax_whole(density, gradient)
    return density, omega_squared
```

```python
import functools

import jax
import jax.numpy as jnp
from jax import lax
from jax.experimental import pallas as pl
from jax.experimental.pallas import tpu as pltpu
from jax.sharding import PartitionSpec as P

SWEEPS = 8
FILTER_WEIGHT = 4.0
W = SWEEPS
MESH = pl.DeviceIdType.MESH
SIDES = tuple((dx, dy) for dx in (-1, 0, 1) for dy in (-1, 0, 1) if (dx, dy) != (0, 0))


def kernel(n_gx, n_ka, modes, perm_hbm, phase, edge, out, omega,
           fields, halo, perm, inv, part, recv, gpad, dens, norm_msg, energy_msg, weight, energy, rot,
           load_sem, perm_sem, halo_send, halo_recv, norm_send, norm_recv, energy_send, energy_recv,
           red_send, red_recv, side_send, side_recv):
    K, B, _, _, PL, NY, NZ = fields.shape
    R = NY // n_ka
    M = K * B
    gx = lax.axis_index("gx")
    ka = lax.axis_index("ka")

    def gx_at(d):
        return lax.rem(gx + d + n_gx, n_gx)

    def ka_at(d):
        return lax.rem(ka + d + n_ka, n_ka)

    loads = [pltpu.make_async_copy(modes.at[m // B, m % B], fields.at[m // B, m % B], load_sem.at[m]) for m in range(M)]
    for c in loads:
        c.start()
    perm_load = pltpu.make_async_copy(perm_hbm, perm, perm_sem)
    perm_load.start()

    barrier = pltpu.get_barrier_semaphore()
    partners = [(d, 0) for d in range(1, n_gx)] + [(0, d) for d in range(1, n_ka)] + [s for s in SIDES if 0 not in s]
    for dx, dy in partners:
        pl.semaphore_signal(barrier, inc=1, device_id={"gx": gx_at(dx), "ka": ka_at(dy)}, device_id_type=MESH)
    pl.semaphore_wait(barrier, len(partners))

    halos = [
        pltpu.make_async_remote_copy(
            src_ref=modes.at[m // B, m % B, :, 1:3, PL - 1], dst_ref=halo.at[m // B, m % B],
            send_sem=halo_send.at[m], recv_sem=halo_recv.at[m],
            device_id={"gx": gx_at(1)}, device_id_type=MESH)
        for m in range(M)
    ]
    for c in halos:
        c.start()

    norm_msg[gx] = jnp.zeros((8, NZ), jnp.float32)
    for m in range(M):
        loads[m].wait()

        def norm_step(p, acc, m=m):
            for ri in range(2):
                for comp in range(3):
                    x = fields[m // B, m % B, ri, comp, p]
                    acc = acc + jnp.sum((x * x).reshape(NY // 8, 8, NZ), axis=0)
            return acc

        acc = lax.fori_loop(0, PL, norm_step, jnp.zeros((8, NZ), jnp.float32))
        norm_msg[gx, m:m + 1] = jnp.sum(acc, axis=0, keepdims=True)

    def exchange(msg, send, recv_sems):
        copies = []
        for d in range(1, n_gx):
            copies.append(pltpu.make_async_remote_copy(
                src_ref=msg.at[gx], dst_ref=msg.at[gx], send_sem=send.at[d], recv_sem=recv_sems.at[gx],
                device_id={"gx": gx_at(d)}, device_id_type=MESH))
        for c in copies:
            c.start()
        return copies

    def gather(msg, send, recv_sems):
        for d in range(1, n_gx):
            src = gx_at(d)
            pltpu.make_async_remote_copy(
                src_ref=msg.at[src], dst_ref=msg.at[src], send_sem=send.at[d], recv_sem=recv_sems.at[src],
                device_id={"gx": src}, device_id_type=MESH).wait_recv()
        total = msg[0]
        for i in range(1, n_gx):
            total = total + msg[i]
        return jnp.broadcast_to(jnp.sum(total, axis=1, keepdims=True), (8, NZ))

    norm_copies = exchange(norm_msg, norm_send, norm_recv)

    perm_load.wait()

    def inverse_step(p, carry):
        inv[p] = 1.0 / perm[p]
        return carry

    lax.fori_loop(0, PL, inverse_step, 0)
    for k in range(K):
        angle = jnp.full((8, NZ), phase[k], jnp.float32)
        rot[k, 0] = jnp.where(gx == 0, jnp.cos(angle), 1.0)
        rot[k, 1] = jnp.where(gx == 0, jnp.sin(angle), 0.0)
    energy[...] = jnp.zeros_like(energy)

    norms = gather(norm_msg, norm_send, norm_recv)
    cells = float(n_gx * PL * NY * NZ)
    for m in range(M):
        sign = 1.0 - 2.0 * edge[m // B, m % B].astype(jnp.float32)
        weight[m] = jnp.broadcast_to(sign * cells / norms[m:m + 1], (8, NZ))

    first_lane = lax.broadcasted_iota(jnp.int32, (R, NZ), 1) == 0
    last_lane = lax.broadcasted_iota(jnp.int32, (W + R + W, NZ), 1) == NZ - 1
    first_lane_wide = lax.broadcasted_iota(jnp.int32, (W + R + W, NZ), 1) == 0

    def red_copy(p, c):
        return pltpu.make_async_remote_copy(
            src_ref=part.at[c, p], dst_ref=recv.at[ka, p], send_sem=red_send.at[c, p], recv_sem=red_recv.at[ka, p],
            device_id={"ka": c}, device_id_type=MESH)

    def chunk(p, c, first):
        r0 = pl.multiple_of(c * R, R)
        rows = pl.ds(r0, R)
        before = pl.ds(pl.multiple_of(lax.rem(r0 + NY - 8, NY), 8), 8)
        inverse = inv[p, rows]
        total = jnp.zeros((R, NZ), jnp.float32)
        tile = lambda a: jnp.concatenate([a] * (R // 8), axis=0)
        for m in range(M):
            k, b = m // B, m % B
            square = None
            if first:
                cosine, sine = tile(rot[k, 0]), tile(rot[k, 1])
                old = [[halo[k, b, ri, comp, rows] for comp in range(2)] for ri in range(2)]
                low = [[old[0][comp] * cosine + old[1][comp] * sine for comp in range(2)],
                       [old[1][comp] * cosine - old[0][comp] * sine for comp in range(2)]]
            for ri in range(2):
                hx, hy, hz = [fields[k, b, ri, comp, p, rows] for comp in range(3)]
                if first:
                    hy_low, hz_low = low[ri]
                else:
                    hy_low, hz_low = [fields[k, b, ri, comp, p - 1, rows] for comp in (1, 2)]

                def below(comp, h):
                    both = jnp.concatenate([fields[k, b, ri, comp, p, before], h], axis=0)
                    return pltpu.roll(both, 1, 0)[8:]

                def lower(h):
                    return jnp.where(first_lane, 0.0, pltpu.roll(h, 1, 1))

                curl_x = (hz - below(2, hz)) - (hy - lower(hy))
                curl_y = (hx - lower(hx)) - (hz - hz_low)
                curl_z = (hy - hy_low) - (hx - below(0, hx))
                value = curl_x * curl_x + curl_y * curl_y + curl_z * curl_z
                square = value if square is None else square + value
            energy[m] += jnp.sum((square * inverse).reshape(R // 8, 8, NZ), axis=0)
            total = total + tile(weight[m]) * square
        part[c, p] = total * inverse * inverse

        @pl.when(c != ka)
        def _():
            red_copy(p, c).start()

    def stage_a(i, carry):
        chunk(1 + i // n_ka, lax.rem(i, n_ka), False)
        return carry

    lax.fori_loop(0, (PL - 1) * n_ka, stage_a, 0)

    for c in halos:
        c.wait_recv()

    def stage_b(c, carry):
        chunk(0, c, True)
        return carry

    lax.fori_loop(0, n_ka, stage_b, 0)

    energy_msg[gx] = jnp.zeros((8, NZ), jnp.float32)
    for m in range(M):
        energy_msg[gx, m:m + 1] = jnp.sum(energy[m], axis=0, keepdims=True)
    energy_copies = exchange(energy_msg, energy_send, energy_recv)

    def gathered(p):
        total = part[ka, p]
        for d in range(1, n_ka):
            src = ka_at(d)
            pltpu.make_async_remote_copy(
                src_ref=part.at[src, p], dst_ref=recv.at[src, p], send_sem=red_send.at[src, p],
                recv_sem=red_recv.at[src, p], device_id={"ka": src}, device_id_type=MESH).wait_recv()
            total = total + recv[src, p]
        gpad[W + p, W:W + R] = total

    def side_copies(stage, p0, planes):
        copies = []
        for i, (dx, dy) in enumerate(SIDES):
            rows = R if dy == 0 else W
            src_row = {0: W, 1: R, -1: W}[dy]
            dst_row = {0: W, 1: 0, -1: W + R}[dy]
            copies.append(pltpu.make_async_remote_copy(
                src_ref=gpad.at[pl.ds(W + p0, planes), pl.ds(src_row, rows)],
                dst_ref=gpad.at[pl.ds(W - dx * PL + p0, planes), pl.ds(dst_row, rows)],
                send_sem=side_send.at[stage, i], recv_sem=side_recv.at[stage, i],
                device_id={"gx": gx_at(dx), "ka": ka_at(dy)}, device_id_type=MESH))
        for c in copies:
            c.start()
        return copies

    def gather_step(p, carry):
        gathered(p)
        return carry

    lax.fori_loop(1, PL, gather_step, 0)
    sides = side_copies(0, 1, PL - 1)
    gathered(0)
    sides += side_copies(1, 0, 1)
    for c in sides:
        c.wait_recv()

    scale = 1.0 / (1.0 + 6.0 * FILTER_WEIGHT)
    for sweep in range(1, SWEEPS + 1):
        source = gpad if sweep == 1 else dens.at[sweep % 2]
        target = dens.at[(sweep + 1) % 2]

        def relax(p, carry, sweep=sweep, source=source, target=target):
            under, center = carry
            over = source[p + 1]
            near = under + over + pltpu.roll(center, 1, 0) + pltpu.roll(center, W + R + W - 1, 0)
            near = near + jnp.where(first_lane_wide, 0.0, pltpu.roll(center, 1, 1))
            near = near + jnp.where(last_lane, 0.0, pltpu.roll(center, NZ - 1, 1))
            value = (gpad[p] + FILTER_WEIGHT * near) * scale
            if sweep == SWEEPS:
                out[p - W] = value[W:W + R]
            else:
                target[p] = value
            return center, over

        lax.fori_loop(sweep, 2 * W + PL - sweep, relax, (source[sweep - 1], source[sweep]))

    energies = gather(energy_msg, energy_send, energy_recv)
    ratio = energies / norms
    for m in range(M):
        omega[m // B, m % B] = ratio[m, 0]

    for c in halos + norm_copies + energy_copies + sides:
        c.wait_send()

    def sent(p, carry):
        for d in range(1, n_ka):
            red_copy(p, ka_at(d)).wait_send()
        return carry

    lax.fori_loop(0, PL, sent, 0)


def shards(n_gx, n_ka, bloch_modes, permittivity, bloch_phase, edge_side):
    K, B, _, _, PL, NY, NZ = bloch_modes.shape
    R = NY // n_ka
    assert PL == W and R >= W
    M = K * B
    f32 = jnp.float32
    dma = pltpu.SemaphoreType.DMA
    return pl.pallas_call(
        functools.partial(kernel, n_gx, n_ka),
        out_shape=(jax.ShapeDtypeStruct((PL, R, NZ), f32), jax.ShapeDtypeStruct((K, B), f32)),
        in_specs=[pl.BlockSpec(memory_space=pl.ANY), pl.BlockSpec(memory_space=pl.ANY),
                  pl.BlockSpec(memory_space=pltpu.SMEM), pl.BlockSpec(memory_space=pltpu.SMEM)],
        out_specs=(pl.BlockSpec(memory_space=pltpu.VMEM), pl.BlockSpec(memory_space=pltpu.SMEM)),
        scratch_shapes=[
            pltpu.VMEM((K, B, 2, 3, PL, NY, NZ), f32),
            pltpu.VMEM((K, B, 2, 2, NY, NZ), f32),
            pltpu.VMEM((PL, NY, NZ), f32),
            pltpu.VMEM((PL, NY, NZ), f32),
            pltpu.VMEM((n_ka, PL, R, NZ), f32),
            pltpu.VMEM((n_ka, PL, R, NZ), f32),
            pltpu.VMEM((PL + 2 * W, R + 2 * W, NZ), f32),
            pltpu.VMEM((2, PL + 2 * W, R + 2 * W, NZ), f32),
            pltpu.VMEM((n_gx, 8, NZ), f32),
            pltpu.VMEM((n_gx, 8, NZ), f32),
            pltpu.VMEM((M, 8, NZ), f32),
            pltpu.VMEM((M, 8, NZ), f32),
            pltpu.VMEM((K, 2, 8, NZ), f32),
            dma((M,)), dma, dma((M,)), dma((M,)),
            dma((n_gx,)), dma((n_gx,)), dma((n_gx,)), dma((n_gx,)),
            dma((n_ka, PL)), dma((n_ka, PL)), dma((2, len(SIDES))), dma((2, len(SIDES))),
        ],
        compiler_params=pltpu.CompilerParams(
            collective_id=0, has_side_effects=True, vmem_limit_bytes=48 * 1024 * 1024),
    )(bloch_modes, permittivity, bloch_phase, edge_side)


def solution(mesh):
    return jax.shard_map(
        functools.partial(shards, mesh.shape["gx"], mesh.shape["ka"]),
        mesh=mesh,
        in_specs=(
            P(("parts", "ka"), None, None, None, "gx", None, None),
            P(("parts", "gx"), None, None),
            P("ka"),
            P("ka", None),
        ),
        out_specs=(P(("parts", "gx"), "ka", None), P(("parts", "ka"), None)),
        check_vma=False,
    )
```

```python
import functools

import jax
import jax.numpy as jnp
from jax import lax
from jax.experimental import pallas as pl
from jax.experimental.pallas import tpu as pltpu
from jax.sharding import PartitionSpec as P

SWEEPS = 8
FILTER_WEIGHT = 4.0
W = SWEEPS
MESH = pl.DeviceIdType.MESH
PLANES = 2


def kernel(n_gx, n_ka, modes, perm_hbm, phase_hbm, edge_hbm, out_hbm, omega_hbm,
           fields, halo, perm, inv, part, recv, gpad, dens_a, dens_b, out, omega, phase, edge, norm_msg, energy_msg, weight, energy, rot,
           load_sem, perm_sem, small_sem, out_sem, halo_send, halo_recv, norm_send, norm_recv, energy_send, energy_recv,
           red_send, red_recv, side_send, side_recv):
    K, B, _, _, PL, NY, NZ = fields.shape
    R = NY // n_ka
    M = K * B
    gx = lax.axis_index("gx")
    ka = lax.axis_index("ka")

    def gx_at(d):
        return lax.rem(gx + d + n_gx, n_gx)

    def ka_at(d):
        return lax.rem(ka + d + n_ka, n_ka)

    loads = [pltpu.make_async_copy(modes.at[m // B, m % B], fields.at[m // B, m % B], load_sem.at[m]) for m in range(M)]
    for c in loads:
        c.start()
    perm_load = pltpu.make_async_copy(perm_hbm, perm, perm_sem)
    perm_load.start()
    small_loads = [pltpu.make_async_copy(phase_hbm, phase, small_sem.at[0]),
                   pltpu.make_async_copy(edge_hbm, edge, small_sem.at[1])]
    for c in small_loads:
        c.start()

    barrier = pltpu.get_barrier_semaphore()
    partners = [(d, 0) for d in range(1, n_gx)] + [(0, d) for d in range(1, n_ka)]
    for dx, dy in partners:
        pl.semaphore_signal(barrier, inc=1, device_id={"gx": gx_at(dx), "ka": ka_at(dy)}, device_id_type=MESH)
    pl.semaphore_wait(barrier, len(partners))

    halos = [
        pltpu.make_async_remote_copy(
            src_ref=modes.at[m // B, m % B, :, 1:3, PL - 1], dst_ref=halo.at[m // B, m % B],
            send_sem=halo_send.at[m], recv_sem=halo_recv.at[m],
            device_id={"gx": gx_at(1)}, device_id_type=MESH)
        for m in range(M)
    ]
    early = 1
    for c in halos[:early]:
        c.start()

    norm_msg[gx] = jnp.zeros((8, NZ), jnp.float32)
    for m in range(M):
        loads[m].wait()

        def norm_step(p, acc, m=m):
            for ri in range(2):
                for comp in range(3):
                    x = fields[m // B, m % B, ri, comp, p]
                    acc = acc + jnp.sum((x * x).reshape(NY // 8, 8, NZ), axis=0)
            return acc

        acc = lax.fori_loop(0, PL, norm_step, jnp.zeros((8, NZ), jnp.float32))
        norm_msg[gx, m:m + 1] = jnp.sum(acc, axis=0, keepdims=True)

    def exchange(msg, send, recv_sems):
        copies = []
        for d in range(1, n_gx):
            copies.append(pltpu.make_async_remote_copy(
                src_ref=msg.at[gx], dst_ref=msg.at[gx], send_sem=send.at[d], recv_sem=recv_sems.at[gx],
                device_id={"gx": gx_at(d)}, device_id_type=MESH))
        for c in copies:
            c.start()
        return copies

    def gather(msg, send, recv_sems):
        for d in range(1, n_gx):
            src = gx_at(d)
            pltpu.make_async_remote_copy(
                src_ref=msg.at[src], dst_ref=msg.at[src], send_sem=send.at[d], recv_sem=recv_sems.at[src],
                device_id={"gx": src}, device_id_type=MESH).wait_recv()
        total = msg[0]
        for i in range(1, n_gx):
            total = total + msg[i]
        return jnp.broadcast_to(jnp.sum(total, axis=1, keepdims=True), (8, NZ))

    norm_copies = exchange(norm_msg, norm_send, norm_recv)
    for c in halos[early:]:
        c.start()

    for c in [perm_load] + small_loads:
        c.wait()

    def inverse_step(p, carry):
        inv[p] = 1.0 / perm[p]
        return carry

    lax.fori_loop(0, PL, inverse_step, 0)
    for k in range(K):
        angle = jnp.full((8, NZ), phase[k], jnp.float32)
        rot[k, 0] = jnp.where(gx == 0, jnp.cos(angle), 1.0)
        rot[k, 1] = jnp.where(gx == 0, jnp.sin(angle), 0.0)
    energy[...] = jnp.zeros_like(energy)

    norms = gather(norm_msg, norm_send, norm_recv)
    cells = float(n_gx * PL * NY * NZ)
    for m in range(M):
        sign = 1.0 - 2.0 * edge[m // B, m % B].astype(jnp.float32)
        weight[m] = jnp.broadcast_to(sign * cells / norms[m:m + 1], (8, NZ))

    first_lane = lax.broadcasted_iota(jnp.int32, (R, NZ), 1) == 0
    last_lane = lax.broadcasted_iota(jnp.int32, (PLANES, W + R + W, NZ), 2) == NZ - 1
    first_lane_wide = lax.broadcasted_iota(jnp.int32, (PLANES, W + R + W, NZ), 2) == 0

    def red_copy(p, c):
        return pltpu.make_async_remote_copy(
            src_ref=part.at[c, p], dst_ref=recv.at[ka, p], send_sem=red_send.at[c, p], recv_sem=red_recv.at[ka, p],
            device_id={"ka": c}, device_id_type=MESH)

    def chunk(p, c, first):
        r0 = pl.multiple_of(c * R, R)
        rows = pl.ds(r0, R)
        before = pl.ds(pl.multiple_of(lax.rem(r0 + NY - 8, NY), 8), 8)
        inverse = inv[p, rows]
        total = jnp.zeros((R, NZ), jnp.float32)
        tile = lambda a: jnp.concatenate([a] * (R // 8), axis=0)
        for m in range(M):
            k, b = m // B, m % B
            square = None
            if first:
                cosine, sine = tile(rot[k, 0]), tile(rot[k, 1])
                old = [[halo[k, b, ri, comp, rows] for comp in range(2)] for ri in range(2)]
                low = [[old[0][comp] * cosine + old[1][comp] * sine for comp in range(2)],
                       [old[1][comp] * cosine - old[0][comp] * sine for comp in range(2)]]
            for ri in range(2):
                hx, hy, hz = [fields[k, b, ri, comp, p, rows] for comp in range(3)]
                if first:
                    hy_low, hz_low = low[ri]
                else:
                    hy_low, hz_low = [fields[k, b, ri, comp, p - 1, rows] for comp in (1, 2)]

                def below(comp, h):
                    both = jnp.concatenate([fields[k, b, ri, comp, p, before], h], axis=0)
                    return pltpu.roll(both, 1, 0)[8:]

                def lower(h):
                    return jnp.where(first_lane, 0.0, pltpu.roll(h, 1, 1))

                curl_x = (hz - below(2, hz)) - (hy - lower(hy))
                curl_y = (hx - lower(hx)) - (hz - hz_low)
                curl_z = (hy - hy_low) - (hx - below(0, hx))
                value = curl_x * curl_x + curl_y * curl_y + curl_z * curl_z
                square = value if square is None else square + value
            energy[m] += jnp.sum((square * inverse).reshape(R // 8, 8, NZ), axis=0)
            total = total + tile(weight[m]) * square
        part[c, p] = total * inverse * inverse

        @pl.when(c != ka)
        def _():
            red_copy(p, c).start()

    def stage_a(i, carry):
        chunk(1 + i // n_ka, lax.rem(i, n_ka), False)
        return carry

    lax.fori_loop(0, (PL - 1) * n_ka, stage_a, 0)

    for c in halos:
        c.wait_recv()

    def stage_b(c, carry):
        chunk(0, c, True)
        return carry

    lax.fori_loop(0, n_ka, stage_b, 0)

    energy_msg[gx] = jnp.zeros((8, NZ), jnp.float32)
    for m in range(M):
        energy_msg[gx, m:m + 1] = jnp.sum(energy[m], axis=0, keepdims=True)
    energy_copies = exchange(energy_msg, energy_send, energy_recv)

    def gathered(p):
        total = part[ka, p]
        for d in range(1, n_ka):
            src = ka_at(d)
            pltpu.make_async_remote_copy(
                src_ref=part.at[src, p], dst_ref=recv.at[src, p], send_sem=red_send.at[src, p],
                recv_sem=red_recv.at[src, p], device_id={"ka": src}, device_id_type=MESH).wait_recv()
            total = total + recv[src, p]
        gpad[W + p, W:W + R] = total

    def side_copies(stage, sides, p0, planes):
        copies = []
        for i, (dx, dy, row, dst, rows) in enumerate(sides):
            copies.append(pltpu.make_async_remote_copy(
                src_ref=gpad.at[pl.ds(W + p0, planes), pl.ds(row, rows)],
                dst_ref=gpad.at[pl.ds(W - dx * PL + p0, planes), pl.ds(dst, rows)],
                send_sem=side_send.at[stage, i], recv_sem=side_recv.at[stage, i],
                device_id={"gx": gx_at(dx), "ka": ka_at(dy)}, device_id_type=MESH))
        for c in copies:
            c.start()
        return copies

    faces = ((0, 1, R, 0, W), (0, -1, W, W + R, W), (1, 0, W, W, R), (-1, 0, W, W, R))
    corners = tuple((dx, 0, row, row, W) for dx in (1, -1) for row in (0, W + R))

    def gather_step(p, carry):
        gathered(p)
        return carry

    lax.fori_loop(1, PL, gather_step, 0)
    sides = side_copies(0, faces, 1, PL - 1)
    gathered(0)
    sides += side_copies(1, faces, 0, 1)
    for c in (sides[0], sides[1], sides[4], sides[5]):
        c.wait_recv()
    last = side_copies(2, corners, 0, PL)
    for c in sides[2:4] + sides[6:8] + last:
        c.wait_recv()
    sides += last

    scale = 1.0 / (1.0 + 6.0 * FILTER_WEIGHT)
    rows_all = W + R + W
    for sweep in range(1, SWEEPS + 1):
        source = gpad if sweep == 1 else (dens_a, dens_b)[sweep % 2]
        target = (dens_b, dens_a)[sweep % 2]
        for p in range(sweep, 2 * W + PL - sweep, PLANES):
            center = source[p:p + PLANES]
            near = source[p - 1:p - 1 + PLANES] + source[p + 1:p + 1 + PLANES]
            near = near + pltpu.roll(center, 1, 1) + pltpu.roll(center, rows_all - 1, 1)
            near = near + jnp.where(first_lane_wide, 0.0, pltpu.roll(center, 1, 2))
            near = near + jnp.where(last_lane, 0.0, pltpu.roll(center, NZ - 1, 2))
            value = (gpad[p:p + PLANES] + FILTER_WEIGHT * near) * scale
            if sweep == SWEEPS:
                out[p - W:p - W + PLANES] = value[:, W:W + R]
            else:
                target[p:p + PLANES] = value
    out_copy = pltpu.make_async_copy(out, out_hbm, out_sem.at[0])
    out_copy.start()

    energies = gather(energy_msg, energy_send, energy_recv)
    ratio = energies / norms
    for m in range(M):
        omega[m // B, m % B] = ratio[m, 0]
    omega_copy = pltpu.make_async_copy(omega, omega_hbm, out_sem.at[1])
    omega_copy.start()
    out_copy.wait()
    omega_copy.wait()

    for c in halos + norm_copies + energy_copies + sides:
        c.wait_send()

    def sent(p, carry):
        for d in range(1, n_ka):
            red_copy(p, ka_at(d)).wait_send()
        return carry

    lax.fori_loop(0, PL, sent, 0)


def shards(n_gx, n_ka, bloch_modes, permittivity, bloch_phase, edge_side):
    K, B, _, _, PL, NY, NZ = bloch_modes.shape
    R = NY // n_ka
    assert PL == W and R >= W
    M = K * B
    f32 = jnp.float32
    dma = pltpu.SemaphoreType.DMA
    return pl.pallas_call(
        functools.partial(kernel, n_gx, n_ka),
        out_shape=(jax.ShapeDtypeStruct((PL, R, NZ), f32), jax.ShapeDtypeStruct((K, B), f32)),
        in_specs=[pl.BlockSpec(memory_space=pltpu.HBM)] * 4,
        out_specs=(pl.BlockSpec(memory_space=pltpu.HBM), pl.BlockSpec(memory_space=pltpu.HBM)),
        scratch_shapes=[
            pltpu.VMEM((K, B, 2, 3, PL, NY, NZ), f32),
            pltpu.VMEM((K, B, 2, 2, NY, NZ), f32),
            pltpu.VMEM((PL, NY, NZ), f32),
            pltpu.VMEM((PL, NY, NZ), f32),
            pltpu.VMEM((n_ka, PL, R, NZ), f32),
            pltpu.VMEM((n_ka, PL, R, NZ), f32),
            pltpu.VMEM((PL + 2 * W, R + 2 * W, NZ), f32),
            pltpu.VMEM((PL + 2 * W, R + 2 * W, NZ), f32),
            pltpu.VMEM((PL + 2 * W, R + 2 * W, NZ), f32),
            pltpu.VMEM((PL, R, NZ), f32),
            pltpu.SMEM((K, B), f32),
            pltpu.SMEM((K,), f32),
            pltpu.SMEM((K, B), jnp.int32),
            pltpu.VMEM((n_gx, 8, NZ), f32),
            pltpu.VMEM((n_gx, 8, NZ), f32),
            pltpu.VMEM((M, 8, NZ), f32),
            pltpu.VMEM((M, 8, NZ), f32),
            pltpu.VMEM((K, 2, 8, NZ), f32),
            dma((M,)), dma, dma((2,)), dma((2,)), dma((M,)), dma((M,)),
            dma((n_gx,)), dma((n_gx,)), dma((n_gx,)), dma((n_gx,)),
            dma((n_ka, PL)), dma((n_ka, PL)), dma((3, 4)), dma((3, 4)),
        ],
        compiler_params=pltpu.CompilerParams(
            collective_id=0, has_side_effects=True, vmem_limit_bytes=62 * 1024 * 1024),
    )(bloch_modes, permittivity, bloch_phase, edge_side)


def solution(mesh):
    return jax.shard_map(
        functools.partial(shards, mesh.shape["gx"], mesh.shape["ka"]),
        mesh=mesh,
        in_specs=(
            P(("parts", "ka"), None, None, None, "gx", None, None),
            P(("parts", "gx"), None, None),
            P("ka"),
            P("ka", None),
        ),
        out_specs=(P(("parts", "gx"), "ka", None), P(("parts", "ka"), None)),
        check_vma=False,
    )
```

```python
import functools

import jax
import jax.numpy as jnp
from jax import lax
from jax.experimental import pallas as pl
from jax.experimental.pallas import tpu as pltpu
from jax.sharding import PartitionSpec as P

SWEEPS = 8
FILTER_WEIGHT = 4.0
W = SWEEPS
MESH = pl.DeviceIdType.MESH
PLANES = 2


def kernel(n_gx, n_ka, modes, perm_hbm, phase_hbm, edge_hbm, out_hbm, omega_hbm,
           fields, halo, perm, inv, part, recv, gpad, dens_a, dens_b, out, omega, phase, edge, norm_msg, energy_msg, weight, energy, rot,
           load_sem, perm_sem, small_sem, out_sem, halo_send, halo_recv, norm_send, norm_recv, energy_send, energy_recv,
           red_send, red_recv, side_send, side_recv):
    K, B, _, _, PL, NY, NZ = fields.shape
    R = NY // n_ka
    M = K * B
    gx = lax.axis_index("gx")
    ka = lax.axis_index("ka")

    def gx_at(d):
        return lax.rem(gx + d + n_gx, n_gx)

    def ka_at(d):
        return lax.rem(ka + d + n_ka, n_ka)

    loads = [pltpu.make_async_copy(modes.at[m // B, m % B], fields.at[m // B, m % B], load_sem.at[m]) for m in range(M)]
    for c in loads:
        c.start()
    perm_load = pltpu.make_async_copy(perm_hbm, perm, perm_sem)
    perm_load.start()
    small_loads = [pltpu.make_async_copy(phase_hbm, phase, small_sem.at[0]),
                   pltpu.make_async_copy(edge_hbm, edge, small_sem.at[1])]
    for c in small_loads:
        c.start()

    barrier = pltpu.get_barrier_semaphore()
    partners = [(d, 0) for d in range(1, n_gx)] + [(0, d) for d in range(1, n_ka)]
    for dx, dy in partners:
        pl.semaphore_signal(barrier, inc=1, device_id={"gx": gx_at(dx), "ka": ka_at(dy)}, device_id_type=MESH)
    pl.semaphore_wait(barrier, len(partners))

    halos = [
        pltpu.make_async_remote_copy(
            src_ref=modes.at[m // B, m % B, :, 1:3, PL - 1], dst_ref=halo.at[m // B, m % B],
            send_sem=halo_send.at[m], recv_sem=halo_recv.at[m],
            device_id={"gx": gx_at(1)}, device_id_type=MESH)
        for m in range(M)
    ]
    early = 1
    for c in halos[:early]:
        c.start()

    norm_msg[gx] = jnp.zeros((8, NZ), jnp.float32)
    for m in range(M):
        loads[m].wait()

        def norm_step(p, acc, m=m):
            for ri in range(2):
                for comp in range(3):
                    x = fields[m // B, m % B, ri, comp, p]
                    acc = acc + jnp.sum((x * x).reshape(NY // 8, 8, NZ), axis=0)
            return acc

        acc = lax.fori_loop(0, PL, norm_step, jnp.zeros((8, NZ), jnp.float32))
        norm_msg[gx, m:m + 1] = jnp.sum(acc, axis=0, keepdims=True)

    def exchange(msg, send, recv_sems):
        copies = []
        for d in range(1, n_gx):
            copies.append(pltpu.make_async_remote_copy(
                src_ref=msg.at[gx], dst_ref=msg.at[gx], send_sem=send.at[d], recv_sem=recv_sems.at[gx],
                device_id={"gx": gx_at(d)}, device_id_type=MESH))
        for c in copies:
            c.start()
        return copies

    def gather(msg, send, recv_sems):
        for d in range(1, n_gx):
            src = gx_at(d)
            pltpu.make_async_remote_copy(
                src_ref=msg.at[src], dst_ref=msg.at[src], send_sem=send.at[d], recv_sem=recv_sems.at[src],
                device_id={"gx": src}, device_id_type=MESH).wait_recv()
        total = msg[0]
        for i in range(1, n_gx):
            total = total + msg[i]
        return jnp.broadcast_to(jnp.sum(total, axis=1, keepdims=True), (8, NZ))

    norm_copies = exchange(norm_msg, norm_send, norm_recv)
    for c in halos[early:]:
        c.start()

    for c in [perm_load] + small_loads:
        c.wait()

    def inverse_step(p, carry):
        inv[p] = 1.0 / perm[p]
        return carry

    lax.fori_loop(0, PL, inverse_step, 0)
    for k in range(K):
        angle = jnp.full((8, NZ), phase[k], jnp.float32)
        rot[k, 0] = jnp.where(gx == 0, jnp.cos(angle), 1.0)
        rot[k, 1] = jnp.where(gx == 0, jnp.sin(angle), 0.0)
    energy[...] = jnp.zeros_like(energy)

    norms = gather(norm_msg, norm_send, norm_recv)
    cells = float(n_gx * PL * NY * NZ)
    for m in range(M):
        sign = 1.0 - 2.0 * edge[m // B, m % B].astype(jnp.float32)
        weight[m] = jnp.broadcast_to(sign * cells / norms[m:m + 1], (8, NZ))

    first_lane = lax.broadcasted_iota(jnp.int32, (R, NZ), 1) == 0
    last_lane = lax.broadcasted_iota(jnp.int32, (PLANES, W + R + W, NZ), 2) == NZ - 1
    first_lane_wide = lax.broadcasted_iota(jnp.int32, (PLANES, W + R + W, NZ), 2) == 0

    def red_copy(p, c):
        return pltpu.make_async_remote_copy(
            src_ref=part.at[c, p], dst_ref=recv.at[ka, p], send_sem=red_send.at[c, p], recv_sem=red_recv.at[ka, p],
            device_id={"ka": c}, device_id_type=MESH)

    def chunk(p, c, first):
        r0 = pl.multiple_of(c * R, R)
        rows = pl.ds(r0, R)
        before = pl.ds(pl.multiple_of(lax.rem(r0 + NY - 8, NY), 8), 8)
        inverse = inv[p, rows]
        total = jnp.zeros((R, NZ), jnp.float32)
        tile = lambda a: jnp.concatenate([a] * (R // 8), axis=0)
        for m in range(M):
            k, b = m // B, m % B
            square = None
            if first:
                cosine, sine = tile(rot[k, 0]), tile(rot[k, 1])
                old = [[halo[k, b, ri, comp, rows] for comp in range(2)] for ri in range(2)]
                low = [[old[0][comp] * cosine + old[1][comp] * sine for comp in range(2)],
                       [old[1][comp] * cosine - old[0][comp] * sine for comp in range(2)]]
            for ri in range(2):
                hx, hy, hz = [fields[k, b, ri, comp, p, rows] for comp in range(3)]
                if first:
                    hy_low, hz_low = low[ri]
                else:
                    hy_low, hz_low = [fields[k, b, ri, comp, p - 1, rows] for comp in (1, 2)]

                def below(comp, h):
                    both = jnp.concatenate([fields[k, b, ri, comp, p, before], h], axis=0)
                    return pltpu.roll(both, 1, 0)[8:]

                def lower(h):
                    return jnp.where(first_lane, 0.0, pltpu.roll(h, 1, 1))

                curl_x = (hz - below(2, hz)) - (hy - lower(hy))
                curl_y = (hx - lower(hx)) - (hz - hz_low)
                curl_z = (hy - hy_low) - (hx - below(0, hx))
                value = curl_x * curl_x + curl_y * curl_y + curl_z * curl_z
                square = value if square is None else square + value
            energy[m] += jnp.sum((square * inverse).reshape(R // 8, 8, NZ), axis=0)
            total = total + tile(weight[m]) * square
        part[c, p] = total * inverse * inverse

        @pl.when(c != ka)
        def _():
            red_copy(p, c).start()

    def stage_a(i, carry):
        chunk(1 + i // n_ka, lax.rem(ka + 1 + i, n_ka), False)
        return carry

    lax.fori_loop(0, (PL - 1) * n_ka, stage_a, 0)

    for c in halos:
        c.wait_recv()

    def stage_b(c, carry):
        chunk(0, lax.rem(ka + 1 + c, n_ka), True)
        return carry

    lax.fori_loop(0, n_ka, stage_b, 0)

    energy_msg[gx] = jnp.zeros((8, NZ), jnp.float32)
    for m in range(M):
        energy_msg[gx, m:m + 1] = jnp.sum(energy[m], axis=0, keepdims=True)
    energy_copies = exchange(energy_msg, energy_send, energy_recv)

    def gathered(p):
        total = part[ka, p]
        for d in range(1, n_ka):
            src = ka_at(d)
            pltpu.make_async_remote_copy(
                src_ref=part.at[src, p], dst_ref=recv.at[src, p], send_sem=red_send.at[src, p],
                recv_sem=red_recv.at[src, p], device_id={"ka": src}, device_id_type=MESH).wait_recv()
            total = total + recv[src, p]
        gpad[W + p, W:W + R] = total

    def side_copies(stage, sides, p0, planes):
        copies = []
        for i, (dx, dy, row, dst, rows) in enumerate(sides):
            copies.append(pltpu.make_async_remote_copy(
                src_ref=gpad.at[pl.ds(W + p0, planes), pl.ds(row, rows)],
                dst_ref=gpad.at[pl.ds(W - dx * PL + p0, planes), pl.ds(dst, rows)],
                send_sem=side_send.at[stage, i], recv_sem=side_recv.at[stage, i],
                device_id={"gx": gx_at(dx), "ka": ka_at(dy)}, device_id_type=MESH))
        for c in copies:
            c.start()
        return copies

    faces = ((0, 1, R, 0, W), (0, -1, W, W + R, W), (1, 0, W, W, R), (-1, 0, W, W, R))
    corners = tuple((dx, 0, row, row, W) for dx in (1, -1) for row in (0, W + R))

    def gather_step(p, carry):
        gathered(p)
        return carry

    lax.fori_loop(1, PL, gather_step, 0)
    sides = side_copies(0, faces, 1, PL - 1)
    gathered(0)
    sides += side_copies(1, faces, 0, 1)
    for c in (sides[0], sides[1], sides[4], sides[5]):
        c.wait_recv()
    last = side_copies(2, corners, 0, PL)
    for c in sides[2:4] + sides[6:8] + last:
        c.wait_recv()
    sides += last

    scale = 1.0 / (1.0 + 6.0 * FILTER_WEIGHT)
    rows_all = W + R + W
    for sweep in range(1, SWEEPS + 1):
        source = gpad if sweep == 1 else (dens_a, dens_b)[sweep % 2]
        target = (dens_b, dens_a)[sweep % 2]
        for p in range(sweep, 2 * W + PL - sweep, PLANES):
            center = source[p:p + PLANES]
            near = source[p - 1:p - 1 + PLANES] + source[p + 1:p + 1 + PLANES]
            near = near + pltpu.roll(center, 1, 1) + pltpu.roll(center, rows_all - 1, 1)
            near = near + jnp.where(first_lane_wide, 0.0, pltpu.roll(center, 1, 2))
            near = near + jnp.where(last_lane, 0.0, pltpu.roll(center, NZ - 1, 2))
            value = (gpad[p:p + PLANES] + FILTER_WEIGHT * near) * scale
            if sweep == SWEEPS:
                out[p - W:p - W + PLANES] = value[:, W:W + R]
            else:
                target[p:p + PLANES] = value
    out_copy = pltpu.make_async_copy(out, out_hbm, out_sem.at[0])
    out_copy.start()

    energies = gather(energy_msg, energy_send, energy_recv)
    ratio = energies / norms
    for m in range(M):
        omega[m // B, m % B] = ratio[m, 0]
    omega_copy = pltpu.make_async_copy(omega, omega_hbm, out_sem.at[1])
    omega_copy.start()
    out_copy.wait()
    omega_copy.wait()

    for c in halos + norm_copies + energy_copies + sides:
        c.wait_send()

    def sent(p, carry):
        for d in range(1, n_ka):
            red_copy(p, ka_at(d)).wait_send()
        return carry

    lax.fori_loop(0, PL, sent, 0)


def hand_over(density, omega, density_out, omega_out):
    density_out[...] = density[...]
    for k in range(omega.shape[0]):
        for b in range(omega.shape[1]):
            omega_out[k, b] = omega[k, b]


def shards(n_gx, n_ka, bloch_modes, permittivity, bloch_phase, edge_side):
    K, B, _, _, PL, NY, NZ = bloch_modes.shape
    R = NY // n_ka
    assert PL == W and R >= W
    M = K * B
    f32 = jnp.float32
    dma = pltpu.SemaphoreType.DMA
    held = pl.pallas_call(
        functools.partial(kernel, n_gx, n_ka),
        out_shape=(jax.ShapeDtypeStruct((PL, R, NZ), f32), jax.ShapeDtypeStruct((K, B), f32)),
        in_specs=[pl.BlockSpec(memory_space=pltpu.HBM)] * 4,
        out_specs=(pl.BlockSpec(memory_space=pltpu.HBM), pl.BlockSpec(memory_space=pltpu.HBM)),
        scratch_shapes=[
            pltpu.VMEM((K, B, 2, 3, PL, NY, NZ), f32),
            pltpu.VMEM((K, B, 2, 2, NY, NZ), f32),
            pltpu.VMEM((PL, NY, NZ), f32),
            pltpu.VMEM((PL, NY, NZ), f32),
            pltpu.VMEM((n_ka, PL, R, NZ), f32),
            pltpu.VMEM((n_ka, PL, R, NZ), f32),
            pltpu.VMEM((PL + 2 * W, R + 2 * W, NZ), f32),
            pltpu.VMEM((PL + 2 * W, R + 2 * W, NZ), f32),
            pltpu.VMEM((PL + 2 * W, R + 2 * W, NZ), f32),
            pltpu.VMEM((PL, R, NZ), f32),
            pltpu.SMEM((K, B), f32),
            pltpu.SMEM((K,), f32),
            pltpu.SMEM((K, B), jnp.int32),
            pltpu.VMEM((n_gx, 8, NZ), f32),
            pltpu.VMEM((n_gx, 8, NZ), f32),
            pltpu.VMEM((M, 8, NZ), f32),
            pltpu.VMEM((M, 8, NZ), f32),
            pltpu.VMEM((K, 2, 8, NZ), f32),
            dma((M,)), dma, dma((2,)), dma((2,)), dma((M,)), dma((M,)),
            dma((n_gx,)), dma((n_gx,)), dma((n_gx,)), dma((n_gx,)),
            dma((n_ka, PL)), dma((n_ka, PL)), dma((3, 4)), dma((3, 4)),
        ],
        compiler_params=pltpu.CompilerParams(
            collective_id=0, has_side_effects=True, vmem_limit_bytes=62 * 1024 * 1024),
    )(bloch_modes, permittivity, bloch_phase, edge_side)
    return pl.pallas_call(
        hand_over,
        out_shape=(jax.ShapeDtypeStruct((PL, R, NZ), f32), jax.ShapeDtypeStruct((K, B), f32)),
        in_specs=[pl.BlockSpec(memory_space=pltpu.VMEM), pl.BlockSpec(memory_space=pltpu.SMEM)],
        out_specs=(pl.BlockSpec(memory_space=pltpu.VMEM), pl.BlockSpec(memory_space=pltpu.SMEM)),
    )(*held)


def solution(mesh):
    return jax.shard_map(
        functools.partial(shards, mesh.shape["gx"], mesh.shape["ka"]),
        mesh=mesh,
        in_specs=(
            P(("parts", "ka"), None, None, None, "gx", None, None),
            P(("parts", "gx"), None, None),
            P("ka"),
            P("ka", None),
        ),
        out_specs=(P(("parts", "gx"), "ka", None), P(("parts", "ka"), None)),
        check_vma=False,
    )
```

```python
import functools

import jax
import jax.numpy as jnp
from jax import lax
from jax.experimental import pallas as pl
from jax.experimental.pallas import tpu as pltpu
from jax.sharding import PartitionSpec as P

SWEEPS = 8
FILTER_WEIGHT = 4.0
W = SWEEPS
MESH = pl.DeviceIdType.MESH
PLANES = 2


def kernel(n_gx, n_ka, modes, perm_hbm, phase_hbm, edge_hbm, out_hbm, omega_hbm,
           fields, halo, perm, inv, part, recv, gpad, dens_a, dens_b, out, omega, phase, edge, norm_msg, energy_msg, weight, energy, rot,
           load_sem, perm_sem, small_sem, out_sem, halo_send, halo_recv, norm_send, norm_recv, energy_send, energy_recv,
           red_send, red_recv, side_send, side_recv):
    K, B, _, _, PL, NY, NZ = fields.shape
    R = NY // n_ka
    M = K * B
    gx = lax.axis_index("gx")
    ka = lax.axis_index("ka")

    def gx_at(d):
        return lax.rem(gx + d + n_gx, n_gx)

    def ka_at(d):
        return lax.rem(ka + d + n_ka, n_ka)

    loads = [pltpu.make_async_copy(modes.at[m // B, m % B], fields.at[m // B, m % B], load_sem.at[m]) for m in range(M)]
    for c in loads:
        c.start()
    perm_load = pltpu.make_async_copy(perm_hbm, perm, perm_sem)
    perm_load.start()
    small_loads = [pltpu.make_async_copy(phase_hbm, phase, small_sem.at[0]),
                   pltpu.make_async_copy(edge_hbm, edge, small_sem.at[1])]
    for c in small_loads:
        c.start()

    barrier = pltpu.get_barrier_semaphore()
    partners = [(d, 0) for d in range(1, n_gx)] + [(0, d) for d in range(1, n_ka)]
    for dx, dy in partners:
        pl.semaphore_signal(barrier, inc=1, device_id={"gx": gx_at(dx), "ka": ka_at(dy)}, device_id_type=MESH)
    pl.semaphore_wait(barrier, len(partners))

    halos = [
        pltpu.make_async_remote_copy(
            src_ref=modes.at[m // B, m % B, :, 1:3, PL - 1], dst_ref=halo.at[m // B, m % B],
            send_sem=halo_send.at[m], recv_sem=halo_recv.at[m],
            device_id={"gx": gx_at(1)}, device_id_type=MESH)
        for m in range(M)
    ]
    early = 0
    for c in halos[:early]:
        c.start()

    norm_msg[gx] = jnp.zeros((8, NZ), jnp.float32)
    for m in range(M):
        loads[m].wait()

        def norm_step(p, acc, m=m):
            for ri in range(2):
                for comp in range(3):
                    x = fields[m // B, m % B, ri, comp, p]
                    acc = acc + jnp.sum((x * x).reshape(NY // 8, 8, NZ), axis=0)
            return acc

        acc = lax.fori_loop(0, PL, norm_step, jnp.zeros((8, NZ), jnp.float32))
        norm_msg[gx, m:m + 1] = jnp.sum(acc, axis=0, keepdims=True)

    def exchange(msg, send, recv_sems):
        copies = []
        for d in range(1, n_gx):
            copies.append(pltpu.make_async_remote_copy(
                src_ref=msg.at[gx], dst_ref=msg.at[gx], send_sem=send.at[d], recv_sem=recv_sems.at[gx],
                device_id={"gx": gx_at(d)}, device_id_type=MESH))
        for c in copies:
            c.start()
        return copies

    def gather(msg, send, recv_sems):
        for d in range(1, n_gx):
            src = gx_at(d)
            pltpu.make_async_remote_copy(
                src_ref=msg.at[src], dst_ref=msg.at[src], send_sem=send.at[d], recv_sem=recv_sems.at[src],
                device_id={"gx": src}, device_id_type=MESH).wait_recv()
        total = msg[0]
        for i in range(1, n_gx):
            total = total + msg[i]
        return jnp.broadcast_to(jnp.sum(total, axis=1, keepdims=True), (8, NZ))

    norm_copies = exchange(norm_msg, norm_send, norm_recv)
    for c in halos[early:]:
        c.start()

    for c in [perm_load] + small_loads:
        c.wait()

    def inverse_step(p, carry):
        inv[p] = 1.0 / perm[p]
        return carry

    lax.fori_loop(0, PL, inverse_step, 0)
    for k in range(K):
        angle = jnp.full((8, NZ), phase[k], jnp.float32)
        rot[k, 0] = jnp.where(gx == 0, jnp.cos(angle), 1.0)
        rot[k, 1] = jnp.where(gx == 0, jnp.sin(angle), 0.0)
    energy[...] = jnp.zeros_like(energy)

    norms = gather(norm_msg, norm_send, norm_recv)
    cells = float(n_gx * PL * NY * NZ)
    for m in range(M):
        sign = 1.0 - 2.0 * edge[m // B, m % B].astype(jnp.float32)
        weight[m] = jnp.broadcast_to(sign * cells / norms[m:m + 1], (8, NZ))

    first_lane = lax.broadcasted_iota(jnp.int32, (R, NZ), 1) == 0
    last_lane = lax.broadcasted_iota(jnp.int32, (PLANES, W + R + W, NZ), 2) == NZ - 1
    first_lane_wide = lax.broadcasted_iota(jnp.int32, (PLANES, W + R + W, NZ), 2) == 0

    def red_copy(p, c):
        return pltpu.make_async_remote_copy(
            src_ref=part.at[c, p], dst_ref=recv.at[ka, p], send_sem=red_send.at[c, p], recv_sem=red_recv.at[ka, p],
            device_id={"ka": c}, device_id_type=MESH)

    def chunk(p, c, first):
        r0 = pl.multiple_of(c * R, R)
        rows = pl.ds(r0, R)
        before = pl.ds(pl.multiple_of(lax.rem(r0 + NY - 8, NY), 8), 8)
        inverse = inv[p, rows]
        total = jnp.zeros((R, NZ), jnp.float32)
        tile = lambda a: jnp.concatenate([a] * (R // 8), axis=0)
        for m in range(M):
            k, b = m // B, m % B
            square = None
            if first:
                cosine, sine = tile(rot[k, 0]), tile(rot[k, 1])
                old = [[halo[k, b, ri, comp, rows] for comp in range(2)] for ri in range(2)]
                low = [[old[0][comp] * cosine + old[1][comp] * sine for comp in range(2)],
                       [old[1][comp] * cosine - old[0][comp] * sine for comp in range(2)]]
            for ri in range(2):
                hx, hy, hz = [fields[k, b, ri, comp, p, rows] for comp in range(3)]
                if first:
                    hy_low, hz_low = low[ri]
                else:
                    hy_low, hz_low = [fields[k, b, ri, comp, p - 1, rows] for comp in (1, 2)]

                def below(comp, h):
                    both = jnp.concatenate([fields[k, b, ri, comp, p, before], h], axis=0)
                    return pltpu.roll(both, 1, 0)[8:]

                def lower(h):
                    return jnp.where(first_lane, 0.0, pltpu.roll(h, 1, 1))

                curl_x = (hz - below(2, hz)) - (hy - lower(hy))
                curl_y = (hx - lower(hx)) - (hz - hz_low)
                curl_z = (hy - hy_low) - (hx - below(0, hx))
                value = curl_x * curl_x + curl_y * curl_y + curl_z * curl_z
                square = value if square is None else square + value
            energy[m] += jnp.sum((square * inverse).reshape(R // 8, 8, NZ), axis=0)
            total = total + tile(weight[m]) * square
        part[c, p] = total * inverse * inverse

        @pl.when(c != ka)
        def _():
            red_copy(p, c).start()

    def stage_a(i, carry):
        chunk(1 + i // n_ka, lax.rem(ka + 1 + i, n_ka), False)
        return carry

    lax.fori_loop(0, (PL - 1) * n_ka, stage_a, 0)

    for c in halos:
        c.wait_recv()

    def stage_b(c, carry):
        chunk(0, lax.rem(ka + 1 + c, n_ka), True)
        return carry

    lax.fori_loop(0, n_ka, stage_b, 0)

    energy_msg[gx] = jnp.zeros((8, NZ), jnp.float32)
    for m in range(M):
        energy_msg[gx, m:m + 1] = jnp.sum(energy[m], axis=0, keepdims=True)
    energy_copies = exchange(energy_msg, energy_send, energy_recv)

    def gathered(p):
        total = part[ka, p]
        for d in range(1, n_ka):
            src = ka_at(d)
            pltpu.make_async_remote_copy(
                src_ref=part.at[src, p], dst_ref=recv.at[src, p], send_sem=red_send.at[src, p],
                recv_sem=red_recv.at[src, p], device_id={"ka": src}, device_id_type=MESH).wait_recv()
            total = total + recv[src, p]
        gpad[W + p, W:W + R] = total

    def side_copies(stage, sides, p0, planes):
        copies = []
        for i, (dx, dy, row, dst, rows) in enumerate(sides):
            copies.append(pltpu.make_async_remote_copy(
                src_ref=gpad.at[pl.ds(W + p0, planes), pl.ds(row, rows)],
                dst_ref=gpad.at[pl.ds(W - dx * PL + p0, planes), pl.ds(dst, rows)],
                send_sem=side_send.at[stage, i], recv_sem=side_recv.at[stage, i],
                device_id={"gx": gx_at(dx), "ka": ka_at(dy)}, device_id_type=MESH))
        for c in copies:
            c.start()
        return copies

    faces = ((0, 1, R, 0, W), (0, -1, W, W + R, W), (1, 0, W, W, R), (-1, 0, W, W, R))
    corners = tuple((dx, 0, row, row, W) for dx in (1, -1) for row in (0, W + R))

    def gather_step(p, carry):
        gathered(p)
        return carry

    lax.fori_loop(1, PL, gather_step, 0)
    sides = side_copies(0, faces, 1, PL - 1)
    gathered(0)
    sides += side_copies(1, faces, 0, 1)
    for c in (sides[0], sides[1], sides[4], sides[5]):
        c.wait_recv()
    last = side_copies(2, corners, 0, PL)
    for c in sides[2:4] + sides[6:8] + last:
        c.wait_recv()
    sides += last

    scale = 1.0 / (1.0 + 6.0 * FILTER_WEIGHT)
    rows_all = W + R + W
    for sweep in range(1, SWEEPS + 1):
        source = gpad if sweep == 1 else (dens_a, dens_b)[sweep % 2]
        target = (dens_b, dens_a)[sweep % 2]
        for p in range(sweep, 2 * W + PL - sweep, PLANES):
            center = source[p:p + PLANES]
            near = source[p - 1:p - 1 + PLANES] + source[p + 1:p + 1 + PLANES]
            near = near + pltpu.roll(center, 1, 1) + pltpu.roll(center, rows_all - 1, 1)
            near = near + jnp.where(first_lane_wide, 0.0, pltpu.roll(center, 1, 2))
            near = near + jnp.where(last_lane, 0.0, pltpu.roll(center, NZ - 1, 2))
            value = (gpad[p:p + PLANES] + FILTER_WEIGHT * near) * scale
            if sweep == SWEEPS:
                out[p - W:p - W + PLANES] = value[:, W:W + R]
            else:
                target[p:p + PLANES] = value
    out_copy = pltpu.make_async_copy(out, out_hbm, out_sem.at[0])
    out_copy.start()

    energies = gather(energy_msg, energy_send, energy_recv)
    ratio = energies / norms
    for m in range(M):
        omega[m // B, m % B] = ratio[m, 0]
    omega_copy = pltpu.make_async_copy(omega, omega_hbm, out_sem.at[1])
    omega_copy.start()
    out_copy.wait()
    omega_copy.wait()

    for c in halos + norm_copies + energy_copies + sides:
        c.wait_send()

    def sent(p, carry):
        for d in range(1, n_ka):
            red_copy(p, ka_at(d)).wait_send()
        return carry

    lax.fori_loop(0, PL, sent, 0)


def hand_over(density, omega, density_out, omega_out):
    density_out[...] = density[...]
    for k in range(omega.shape[0]):
        for b in range(omega.shape[1]):
            omega_out[k, b] = omega[k, b]


def shards(n_gx, n_ka, bloch_modes, permittivity, bloch_phase, edge_side):
    K, B, _, _, PL, NY, NZ = bloch_modes.shape
    R = NY // n_ka
    assert PL == W and R >= W
    M = K * B
    f32 = jnp.float32
    dma = pltpu.SemaphoreType.DMA
    held = pl.pallas_call(
        functools.partial(kernel, n_gx, n_ka),
        out_shape=(jax.ShapeDtypeStruct((PL, R, NZ), f32), jax.ShapeDtypeStruct((K, B), f32)),
        in_specs=[pl.BlockSpec(memory_space=pltpu.HBM)] * 4,
        out_specs=(pl.BlockSpec(memory_space=pltpu.HBM), pl.BlockSpec(memory_space=pltpu.HBM)),
        scratch_shapes=[
            pltpu.VMEM((K, B, 2, 3, PL, NY, NZ), f32),
            pltpu.VMEM((K, B, 2, 2, NY, NZ), f32),
            pltpu.VMEM((PL, NY, NZ), f32),
            pltpu.VMEM((PL, NY, NZ), f32),
            pltpu.VMEM((n_ka, PL, R, NZ), f32),
            pltpu.VMEM((n_ka, PL, R, NZ), f32),
            pltpu.VMEM((PL + 2 * W, R + 2 * W, NZ), f32),
            pltpu.VMEM((PL + 2 * W, R + 2 * W, NZ), f32),
            pltpu.VMEM((PL + 2 * W, R + 2 * W, NZ), f32),
            pltpu.VMEM((PL, R, NZ), f32),
            pltpu.SMEM((K, B), f32),
            pltpu.SMEM((K,), f32),
            pltpu.SMEM((K, B), jnp.int32),
            pltpu.VMEM((n_gx, 8, NZ), f32),
            pltpu.VMEM((n_gx, 8, NZ), f32),
            pltpu.VMEM((M, 8, NZ), f32),
            pltpu.VMEM((M, 8, NZ), f32),
            pltpu.VMEM((K, 2, 8, NZ), f32),
            dma((M,)), dma, dma((2,)), dma((2,)), dma((M,)), dma((M,)),
            dma((n_gx,)), dma((n_gx,)), dma((n_gx,)), dma((n_gx,)),
            dma((n_ka, PL)), dma((n_ka, PL)), dma((3, 4)), dma((3, 4)),
        ],
        compiler_params=pltpu.CompilerParams(
            collective_id=0, has_side_effects=True, vmem_limit_bytes=62 * 1024 * 1024),
    )(bloch_modes, permittivity, bloch_phase, edge_side)
    return pl.pallas_call(
        hand_over,
        out_shape=(jax.ShapeDtypeStruct((PL, R, NZ), f32), jax.ShapeDtypeStruct((K, B), f32)),
        in_specs=[pl.BlockSpec(memory_space=pltpu.VMEM), pl.BlockSpec(memory_space=pltpu.SMEM)],
        out_specs=(pl.BlockSpec(memory_space=pltpu.VMEM), pl.BlockSpec(memory_space=pltpu.SMEM)),
    )(*held)


def solution(mesh):
    return jax.shard_map(
        functools.partial(shards, mesh.shape["gx"], mesh.shape["ka"]),
        mesh=mesh,
        in_specs=(
            P(("parts", "ka"), None, None, None, "gx", None, None),
            P(("parts", "gx"), None, None),
            P("ka"),
            P("ka", None),
        ),
        out_specs=(P(("parts", "gx"), "ka", None), P(("parts", "ka"), None)),
        check_vma=False,
    )
```
